128 devices in a mesh: seq: 32 (over z, x_hi, y), ch: 4 (over x_lo, core).
Axes of the slice: x: 4 (x_hi: 2, x_lo: 2; x = x_hi * 2 + x_lo), y: 4, z: 4, core: 2. Of those that a mesh axis runs over, the one named last changes fastest.
Arguments:
- tokens: bfloat16 [256, 512, 1536], P('seq', None, 'ch'), may hold values from -6 to 6
- gate_values: bfloat16 [256, 512, 1536], P('seq', None, 'ch'), may hold values from -6 to 6
- first_blocks: bfloat16 [256, 512, 512], P('seq'), may hold values from -0.25 to 0.25
- second_blocks: bfloat16 [512, 256, 256], P('seq'), may hold values from -0.375 to 0.375
- cotangent: bfloat16 [512, 256, 1536], P('seq', None, 'ch'), may hold values from -6 to 6
Outputs:
- mixed_output: bfloat16 [512, 256, 1536], P('seq', None, 'ch')
- token_grad: bfloat16 [256, 512, 1536], P('seq', None, 'ch')
- gate_grad: bfloat16 [256, 512, 1536], P('seq', None, 'ch')
- first_grad: bfloat16 [256, 512, 512], P('seq', 'ch')
- second_grad: bfloat16 [512, 256, 256], P(('seq', 'ch'))
The draws below stay inside these ranges and needn't reach their ends.
All inputs are finite; a program needn't handle non-finite values.
Results may differ from the reference program's by a relative error of at most 0.013.
Values may be sent and summed in bfloat16 or wider, within the bound.
No kernel may reach another device: no remote copies, remote signals or barrier semaphores. Data moves between devices by JAX's collectives and lax.ppermute only.
A program may use at most 128 MiB of HBM per device.

```python
import jax
import jax.numpy as jnp
from jax import lax

ROWS = 256
COLS = 512
D = 1536
N_CH = 4


def block_levels(key, extent, cuts, smallest, top_value):
    loudness = 1.0
    for position, shards_of in cuts:
        draws = jax.random.uniform(jax.random.fold_in(jax.random.fold_in(key, 6), position), (shards_of,), jnp.float32, smallest / len(cuts), top_value / len(cuts))
        loudness = loudness * jnp.repeat(jnp.exp(draws), extent[position] // shards_of).reshape((-1,) + (1,) * (len(extent) - 1 - position))
    return loudness


def bell_draw(stream_key, dims, deviation, bound, pieces=(), held_as=jnp.bfloat16):
    level = block_levels(stream_key, dims, pieces, -0.22, 0.18) if pieces else 1.0
    entries = jax.random.normal(stream_key, dims, jnp.float32) * deviation * level
    return jnp.minimum(jnp.maximum(entries, -bound), bound).astype(held_as)


def setup_inputs(seed: int = 0) -> dict:
    key_list = jax.random.split(jax.random.key(seed), 6)
    tokens = bell_draw(key_list[0], (ROWS, COLS, D), 1.0, 6.0, ((0, 32), (2, 4)))
    gate_values = bell_draw(key_list[1], (ROWS, COLS, D), 1.0, 6.0, ((0, 32), (2, 4)))
    first_blocks = bell_draw(key_list[2], (ROWS, COLS, COLS), COLS ** -0.5, 0.25, ((0, 32),))
    second_blocks = bell_draw(key_list[3], (COLS, ROWS, ROWS), ROWS ** -0.5, 0.375, ((0, 32),))
    cotangent = bell_draw(key_list[4], (COLS, ROWS, D), 1.0, 6.0, ((0, 32), (2, 4)))
    return dict(tokens=tokens, gate_values=gate_values, first_blocks=first_blocks, second_blocks=second_blocks, cotangent=cotangent)


def group_product(left, right):
    left_groups = left.reshape(left.shape[0], N_CH, -1).astype(jnp.float32)
    right_groups = right.reshape(right.shape[0], N_CH, -1).astype(jnp.float32)
    terms = jnp.einsum('pgd,qgd->gpq', left_groups, right_groups).astype(jnp.bfloat16)
    terms = lax.optimization_barrier(terms)
    return jnp.sum(terms.astype(jnp.float32), axis=0).astype(jnp.bfloat16)


def reference(tokens, gate_values, first_blocks, second_blocks, cotangent):
    def forward_row(item):
        block, row, gate_row = item
        hidden = jnp.dot(block, row, preferred_element_type=jnp.float32)
        return (hidden * gate_row.astype(jnp.float32)).astype(jnp.bfloat16)

    gated_rows = lax.map(forward_row, (first_blocks, tokens, gate_values))
    grid_cols = jnp.transpose(gated_rows, (1, 0, 2))

    def column_step(item):
        block, column, cot_col = item
        mixed = jnp.dot(block, column, preferred_element_type=jnp.float32).astype(jnp.bfloat16)
        back = jnp.dot(block.T, cot_col, preferred_element_type=jnp.float32).astype(jnp.bfloat16)
        return mixed, back, group_product(cot_col, column)

    mixed_output, back_cols, second_grad = lax.map(column_step, (second_blocks, grid_cols, cotangent))
    grad_rows = jnp.transpose(back_cols, (1, 0, 2))

    def backward_row(item):
        block, row, gate_row, grad_row = item
        hidden = jnp.dot(block, row, preferred_element_type=jnp.float32)
        gate_grad = (grad_row.astype(jnp.float32) * hidden).astype(jnp.bfloat16)
        hidden_grad = (grad_row.astype(jnp.float32) * gate_row.astype(jnp.float32)).astype(jnp.bfloat16)
        token_grad = jnp.dot(block.T, hidden_grad, preferred_element_type=jnp.float32).astype(jnp.bfloat16)
        return token_grad, gate_grad, group_product(hidden_grad, row)

    token_grad, gate_grad, first_grad = lax.map(backward_row, (first_blocks, tokens, gate_values, grad_rows))
    return (mixed_output, token_grad, gate_grad, first_grad, second_grad)
```

```python
import jax
import jax.numpy as jnp
from jax import lax
from jax.experimental import pallas as pl
from jax.experimental.pallas import tpu as pltpu
from jax.sharding import PartitionSpec as P

F32 = jnp.float32
BF16 = jnp.bfloat16
MIB = 1024 * 1024
LANES = 128
PAD = 8

NN = (((1,), (0,)), ((), ()))
NT = (((1,), (1,)), ((), ()))
TN = (((0,), (0,)), ((), ()))

HERE, ACROSS, BESIDE, OPPOSITE = range(4)

GRAD, GATED = range(2)


def dot(a, b, dims):
    return lax.dot_general(a, b, dims, preferred_element_type=F32)


def params(mib=60):
    return pltpu.CompilerParams(vmem_limit_bytes=mib * MIB)


def cost(flops, nbytes):
    return pl.CostEstimate(flops=flops, bytes_accessed=nbytes, transcendentals=0)


def lanes(t):
    return slice(t * LANES, (t + 1) * LANES)


def back_columns(second_blocks, cotangent, devices):
    cols, rows, d = cotangent.shape
    steps, tiles = 2, d // LANES
    span = rows // steps
    pitch = span + PAD
    per = rows // devices

    def kernel(s_ref, g_ref, out_ref, acc):
        for c in range(cols):
            back = dot(s_ref[c], g_ref[c], TN)
            for t in range(tiles):
                acc[t, c * pitch:c * pitch + span, :] = back[:, lanes(t)]

        def device(k, carry):
            for r in range(per):
                for t in range(tiles):
                    strip = acc[t, pl.ds(k * per + r, cols, stride=pitch), :]
                    out_ref[k, 0, r, :, lanes(t)] = strip.astype(BF16)
            return carry

        lax.fori_loop(0, span // per, device, 0, unroll=2)

    return pl.pallas_call(
        kernel,
        grid=(steps,),
        in_specs=[
            pl.BlockSpec((cols, rows, span), lambda i: (0, 0, i)),
            pl.BlockSpec((cols, rows, d), lambda i: (0, 0, 0)),
        ],
        out_specs=pl.BlockSpec((devices // steps, 1, per, cols, d), lambda i: (i, GRAD, 0, 0, 0)),
        out_shape=jax.ShapeDtypeStruct((devices, 2, per, cols, d), BF16),
        scratch_shapes=[pltpu.VMEM((tiles, cols * pitch, LANES), F32)],
        compiler_params=params(),
        cost_estimate=cost(2 * cols * rows * rows * d, 2 * cols * rows * (rows + 2 * d)),
    )(second_blocks, cotangent)


def gated_columns(first_blocks, tokens, gate_values, slabs):
    rows, cols, d = tokens.shape
    devices, _, pairs, both, _ = slabs.shape
    steps, tiles = 4, d // LANES
    span = cols // steps
    pitch = span + PAD

    def kernel(f_ref, t_ref, g_ref, _, out_ref, acc):
        for r in range(rows):
            gated = dot(f_ref[r], t_ref[r], NN) * g_ref[r].astype(F32)
            for t in range(tiles):
                acc[t, r * pitch:r * pitch + span, :] = gated[:, lanes(t)]

        def device(k, carry):
            for j in range(pairs):
                at = 2 * (k * pairs + j)
                for t in range(tiles):
                    even = acc[t, pl.ds(at, rows, stride=pitch), :]
                    odd = acc[t, pl.ds(at + 1, rows, stride=pitch), :]
                    out_ref[k, 0, j, :, lanes(t)] = jnp.concatenate([even, odd], axis=0).astype(BF16)
            return carry

        lax.fori_loop(0, devices // steps, device, 0)

    return pl.pallas_call(
        kernel,
        grid=(steps,),
        in_specs=[
            pl.BlockSpec((rows, span, cols), lambda i: (0, i, 0)),
            pl.BlockSpec((rows, cols, d), lambda i: (0, 0, 0)),
            pl.BlockSpec((rows, span, d), lambda i: (0, i, 0)),
            pl.BlockSpec(memory_space=pl.ANY),
        ],
        out_specs=pl.BlockSpec((devices // steps, 1, pairs, both, d), lambda i: (i, GATED, 0, 0, 0)),
        out_shape=jax.ShapeDtypeStruct(slabs.shape, BF16),
        scratch_shapes=[pltpu.VMEM((tiles, rows * pitch, LANES), F32)],
        input_output_aliases={3: 0},
        compiler_params=params(),
        cost_estimate=cost(2 * rows * cols * cols * d, 2 * rows * cols * (cols + 3 * d)),
    )(first_blocks, tokens, gate_values, slabs)


def grad_spec(slabs, first=0, step=1):
    devices, _, _, both, d = slabs.shape
    return pl.BlockSpec((devices, 1, step, both, d), lambda i: (0, GRAD, first + i, 0, 0))


def first_terms(place, slabs, tokens, gate_values, first, count):
    rows, cols, d = tokens.shape
    part = cols // 4

    def kernel(place_ref, b_ref, t_ref, g_ref, near_ref, far_ref, grad):
        group = b_ref.shape[0] // 4
        outs = (far_ref, far_ref, near_ref, near_ref)
        for k, whose in enumerate((BESIDE, OPPOSITE, HERE, ACROSS)):
            at = place_ref[whose]
            back = b_ref[pl.ds(at * group, group), 0, 0].reshape(part, d).astype(F32)
            gate = g_ref[0, pl.ds(pl.multiple_of(at * part, part), part), :].astype(F32)
            grad[k * part:(k + 1) * part, :] = (back * gate).astype(BF16)
        terms = dot(grad[...], t_ref[0], NT).astype(BF16)
        for k, out in enumerate(outs):
            out[k % 2, 0] = terms[k * part:(k + 1) * part]

    row_spec = pl.BlockSpec((1, cols, d), lambda i: (first + i, 0, 0))
    terms_spec = pl.BlockSpec((2, 1, part, cols), lambda i: (0, i, 0, 0))
    terms_shape = jax.ShapeDtypeStruct((2, count, part, cols), BF16)
    return pl.pallas_call(
        kernel,
        grid=(count,),
        in_specs=[pl.BlockSpec(memory_space=pltpu.SMEM), grad_spec(slabs, first), row_spec, row_spec],
        out_specs=[terms_spec, terms_spec],
        out_shape=[terms_shape, terms_shape],
        scratch_shapes=[pltpu.VMEM((cols, d), BF16)],
        compiler_params=params(24),
        cost_estimate=cost(2 * count * cols * cols * d, 2 * count * cols * (cols + 3 * d)),
    )(place, slabs, tokens, gate_values)


def row_grads(slabs, first_blocks, tokens, gate_values):
    rows, cols, d = tokens.shape

    step = 2

    def kernel(b_ref, f_ref, t_ref, g_ref, tg_ref, gg_ref):
        for k in range(step):
            back = b_ref[:, 0, k].reshape(cols, d).astype(F32)
            hidden_grad = (back * g_ref[k].astype(F32)).astype(BF16)
            tg_ref[k] = dot(f_ref[k], hidden_grad, TN).astype(BF16)
            gg_ref[k] = (back * dot(f_ref[k], t_ref[k], NN)).astype(BF16)

    row_spec = pl.BlockSpec((step, cols, d), lambda i: (i, 0, 0))
    row_shape = jax.ShapeDtypeStruct((rows, cols, d), BF16)
    return pl.pallas_call(
        kernel,
        grid=(rows // step,),
        in_specs=[grad_spec(slabs, 0, step), pl.BlockSpec((step, cols, cols), lambda i: (i, 0, 0)), row_spec, row_spec],
        out_specs=[row_spec, row_spec],
        out_shape=[row_shape, row_shape],
        compiler_params=params(24),
        cost_estimate=cost(4 * rows * cols * cols * d, 2 * rows * cols * (cols + 5 * d)),
    )(slabs, first_blocks, tokens, gate_values)


def column_pair(g_ref, k):
    devices, _, _, both, d = g_ref.shape
    pair = g_ref[:, 0, k].astype(F32).reshape(devices, 2, both // 2, d)
    return [pair[:, c].reshape(devices * both // 2, d).astype(BF16) for c in range(2)]


def second_terms(place, whose, slabs, cotangent):
    cols, rows, d = cotangent.shape
    devices, _, pairs, both, _ = slabs.shape
    step, part = pairs // 4, cols // 4

    def kernel(place_ref, g_ref, c_ref, out_ref):
        for k in range(step):
            for c, column in enumerate(column_pair(g_ref, k)):
                out_ref[0, 2 * k + c] = dot(c_ref[2 * k + c], column, NT).astype(BF16)

    def quarter(i, at):
        return jnp.where(i == 0, at[whose[0]], at[whose[1]])

    return pl.pallas_call(
        kernel,
        grid_spec=pltpu.PrefetchScalarGridSpec(
            num_scalar_prefetch=1,
            grid=(2,),
            in_specs=[
                pl.BlockSpec((devices, 1, step, both, d), lambda i, at: (0, GATED, quarter(i, at), 0, 0)),
                pl.BlockSpec((part, rows, d), lambda i, at: (quarter(i, at), 0, 0)),
            ],
            out_specs=pl.BlockSpec((1, part, rows, rows), lambda i, at: (i, 0, 0, 0)),
        ),
        out_shape=jax.ShapeDtypeStruct((2, part, rows, rows), BF16),
        compiler_params=params(24),
        cost_estimate=cost(cols * rows * rows * d, cols * rows * (rows + 2 * d)),
    )(place, slabs, cotangent)


def mixed_columns(slabs, second_blocks):
    cols, rows, _ = second_blocks.shape
    devices, _, pairs, both, d = slabs.shape
    step = 4

    def kernel(g_ref, s_ref, out_ref):
        for k in range(step):
            for c, column in enumerate(column_pair(g_ref, k)):
                out_ref[2 * k + c] = dot(s_ref[2 * k + c], column, NN).astype(BF16)

    return pl.pallas_call(
        kernel,
        grid=(pairs // step,),
        in_specs=[
            pl.BlockSpec((devices, 1, step, both, d), lambda i: (0, GATED, i, 0, 0)),
            pl.BlockSpec((2 * step, rows, rows), lambda i: (i, 0, 0)),
        ],
        out_specs=pl.BlockSpec((2 * step, rows, d), lambda i: (i, 0, 0)),
        out_shape=jax.ShapeDtypeStruct((cols, rows, d), BF16),
        compiler_params=params(24),
        cost_estimate=cost(2 * cols * rows * rows * d, 2 * cols * rows * (rows + 2 * d)),
    )(slabs, second_blocks)


def swap(x, bit):
    return lax.ppermute(x, "ch", [(i, i ^ bit) for i in range(4)])


def add(a, b):
    return a.astype(F32) + b.astype(F32)


def after(first, *later):
    return lax.optimization_barrier((first, *later))


def local(tokens, gate_values, first_blocks, second_blocks, cotangent):
    rows = tokens.shape[0]
    ch = lax.axis_index("ch")
    place = jnp.stack([ch, ch ^ 2, ch ^ 1, ch ^ 3]).astype(jnp.int32)

    slabs = back_columns(second_blocks, cotangent, lax.axis_size("seq"))
    slabs = gated_columns(first_blocks, tokens, gate_values, slabs)
    slabs, place = after(slabs, place)
    slabs = lax.all_to_all(slabs, "seq", split_axis=0, concat_axis=0, tiled=True)

    def over_cores(near, far):
        return add(near[1], far[1]).astype(BF16)

    def over_chips(near, far, across):
        return (add(near[0], far[0]) + across.astype(F32)).astype(BF16)

    few = rows // 4
    near_a, far_a = first_terms(place, slabs, tokens, gate_values, 0, few)
    far_a = swap(far_a, 1)
    far_c = swap(second_terms(place, (BESIDE, OPPOSITE), slabs, cotangent), 1)
    sum_a, cotangent = after(over_cores(near_a, far_a), cotangent)
    across_a = swap(sum_a, 2)
    near_c = second_terms(place, (HERE, ACROSS), slabs, cotangent)
    across_a, near_c = after(across_a, near_c)
    sum_c, tokens = after(over_cores(near_c, far_c), tokens)
    across_c = swap(sum_c, 2)
    near_b, far_b = first_terms(place, slabs, tokens, gate_values, few, rows - few)
    far_b = swap(far_b, 1)
    across_c, near_b = after(across_c, near_b)
    sum_b, gate_values, second_blocks = after(over_cores(near_b, far_b), gate_values, second_blocks)
    across_b = swap(sum_b, 2)
    mixed_output = mixed_columns(slabs, second_blocks)
    token_grad, gate_grad = row_grads(slabs, first_blocks, tokens, gate_values)
    first_grad = jnp.concatenate([over_chips(near_a, far_a, across_a), over_chips(near_b, far_b, across_b)], axis=0)
    second_grad = over_chips(near_c, far_c, across_c)
    return (mixed_output, token_grad, gate_grad, first_grad, second_grad)


def solution(mesh):
    return jax.shard_map(
        local,
        mesh=mesh,
        in_specs=(
            P("seq", None, "ch"),
            P("seq", None, "ch"),
            P("seq", None, None),
            P("seq", None, None),
            P("seq", None, "ch"),
        ),
        out_specs=(
            P("seq", None, "ch"),
            P("seq", None, "ch"),
            P("seq", None, "ch"),
            P("seq", "ch", None),
            P(("seq", "ch"), None, None),
        ),
        check_vma=False,
    )
```

```python
import jax
import jax.numpy as jnp
from jax import lax
from jax.experimental import pallas as pl
from jax.experimental.pallas import tpu as pltpu
from jax.sharding import PartitionSpec as P

F32 = jnp.float32
BF16 = jnp.bfloat16
MIB = 1024 * 1024
LANES = 128
PAD = 8

NN = (((1,), (0,)), ((), ()))
NT = (((1,), (1,)), ((), ()))
TN = (((0,), (0,)), ((), ()))

HERE, ACROSS, BESIDE, OPPOSITE = range(4)

GRAD, GATED = range(2)


def dot(a, b, dims):
    return lax.dot_general(a, b, dims, preferred_element_type=F32)


def params(mib=60):
    return pltpu.CompilerParams(vmem_limit_bytes=mib * MIB)


def cost(flops, nbytes):
    return pl.CostEstimate(flops=flops, bytes_accessed=nbytes, transcendentals=0)


def lanes(t):
    return slice(t * LANES, (t + 1) * LANES)


def send_slabs(second_blocks, cotangent, first_blocks, tokens, gate_values, devices):
    cols, all_rows, d = cotangent.shape
    rows, all_cols, _ = tokens.shape
    tiles, pairs = d // LANES, cols // 2
    chunk = 4
    chunks = cols // chunk
    back_pitch, gated_pitch = all_rows + PAD, all_cols + PAD

    def kernel(s_hbm, c_hbm, f_hbm, t_hbm, g_hbm, out_ref, s_ref, c_ref, f_ref, t_ref, g_ref, back, gated, sems):
        fetches = []

        def fetch(first, count, *pairs_of_refs):
            for source, target in pairs_of_refs:
                at = pl.ds(first, count)
                copy = pltpu.make_async_copy(source.at[at], target.at[at], sems.at[len(fetches)])
                copy.start()
                fetches.append(copy)

        def arrive(first, count):
            for copy in fetches[first:first + count]:
                copy.wait()

        for i in range(chunks):
            fetch(i * chunk, chunk, (s_hbm, s_ref), (c_hbm, c_ref))
        for r in range(rows):
            fetch(r, 1, (f_hbm, f_ref), (t_hbm, t_ref), (g_hbm, g_ref))

        for i in range(chunks):
            arrive(2 * i, 2)
            for c in range(i * chunk, (i + 1) * chunk):
                product = dot(s_ref[c], c_ref[c], TN)
                for t in range(tiles):
                    back[t, c * back_pitch:c * back_pitch + all_rows, :] = product[:, lanes(t)]

        def rows_of(k, carry):
            for r in range(rows):
                for t in range(tiles):
                    strip = back[t, pl.ds(k * rows + r, cols, stride=back_pitch), :]
                    out_ref[k, GRAD, r, :, lanes(t)] = strip.astype(BF16)
            return carry

        lax.fori_loop(0, devices, rows_of, 0, unroll=2)

        for r in range(rows):
            arrive(2 * chunks + 3 * r, 3)
            product = dot(f_ref[r], t_ref[r], NN) * g_ref[r].astype(F32)
            for t in range(tiles):
                gated[t, r * gated_pitch:r * gated_pitch + all_cols, :] = product[:, lanes(t)]

        def columns_of(k, carry):
            for j in range(pairs):
                at = k * cols + 2 * j
                for t in range(tiles):
                    even = gated[t, pl.ds(at, rows, stride=gated_pitch), :]
                    odd = gated[t, pl.ds(at + 1, rows, stride=gated_pitch), :]
                    out_ref[k, GATED, j, :, lanes(t)] = jnp.concatenate([even, odd], axis=0).astype(BF16)
            return carry

        lax.fori_loop(0, devices, columns_of, 0, unroll=2)

    hbm = pl.BlockSpec(memory_space=pltpu.HBM)
    return pl.pallas_call(
        kernel,
        in_specs=[hbm] * 5,
        out_specs=pl.BlockSpec(memory_space=pltpu.VMEM),
        out_shape=pltpu.VMEM((devices, 2, rows, cols, d), BF16),
        scratch_shapes=[
            pltpu.VMEM(second_blocks.shape, BF16),
            pltpu.VMEM(cotangent.shape, BF16),
            pltpu.VMEM(first_blocks.shape, BF16),
            pltpu.VMEM(tokens.shape, BF16),
            pltpu.VMEM(gate_values.shape, BF16),
            pltpu.VMEM((tiles, cols * back_pitch, LANES), F32),
            pltpu.VMEM((tiles, rows * gated_pitch, LANES), F32),
            pltpu.SemaphoreType.DMA((2 * chunks + 3 * rows,)),
        ],
        compiler_params=params(48),
        cost_estimate=cost(
            2 * cols * all_rows * all_rows * d + 2 * rows * all_cols * all_cols * d,
            2 * cols * all_rows * (all_rows + 2 * d) + 2 * rows * all_cols * (all_cols + 3 * d),
        ),
    )(second_blocks, cotangent, first_blocks, tokens, gate_values)


def grad_spec(slabs, first=0, step=1):
    devices, _, _, both, d = slabs.shape
    return pl.BlockSpec((devices, 1, step, both, d), lambda i: (0, GRAD, first + i, 0, 0))


def first_terms(place, slabs, tokens, gate_values, first, count):
    rows, cols, d = tokens.shape
    part = cols // 4

    def kernel(place_ref, b_ref, t_ref, g_ref, near_ref, far_ref, grad):
        group = b_ref.shape[0] // 4
        outs = (far_ref, far_ref, near_ref, near_ref)
        for k, whose in enumerate((BESIDE, OPPOSITE, HERE, ACROSS)):
            at = place_ref[whose]
            back = b_ref[pl.ds(at * group, group), 0, 0].reshape(part, d).astype(F32)
            gate = g_ref[0, pl.ds(pl.multiple_of(at * part, part), part), :].astype(F32)
            grad[k * part:(k + 1) * part, :] = (back * gate).astype(BF16)
        terms = dot(grad[...], t_ref[0], NT).astype(BF16)
        for k, out in enumerate(outs):
            out[k % 2, 0] = terms[k * part:(k + 1) * part]

    row_spec = pl.BlockSpec((1, cols, d), lambda i: (first + i, 0, 0))
    terms_spec = pl.BlockSpec((2, 1, part, cols), lambda i: (0, i, 0, 0))
    terms_shape = jax.ShapeDtypeStruct((2, count, part, cols), BF16)
    return pl.pallas_call(
        kernel,
        grid=(count,),
        in_specs=[pl.BlockSpec(memory_space=pltpu.SMEM), grad_spec(slabs, first), row_spec, row_spec],
        out_specs=[terms_spec, terms_spec],
        out_shape=[terms_shape, terms_shape],
        scratch_shapes=[pltpu.VMEM((cols, d), BF16)],
        compiler_params=params(24),
        cost_estimate=cost(2 * count * cols * cols * d, 2 * count * cols * (cols + 3 * d)),
    )(place, slabs, tokens, gate_values)


def row_grads(slabs, first_blocks, tokens, gate_values):
    rows, cols, d = tokens.shape

    step = 2

    def kernel(b_ref, f_ref, t_ref, g_ref, tg_ref, gg_ref):
        for k in range(step):
            back = b_ref[:, 0, k].reshape(cols, d).astype(F32)
            hidden_grad = (back * g_ref[k].astype(F32)).astype(BF16)
            tg_ref[k] = dot(f_ref[k], hidden_grad, TN).astype(BF16)
            gg_ref[k] = (back * dot(f_ref[k], t_ref[k], NN)).astype(BF16)

    row_spec = pl.BlockSpec((step, cols, d), lambda i: (i, 0, 0))
    row_shape = jax.ShapeDtypeStruct((rows, cols, d), BF16)
    return pl.pallas_call(
        kernel,
        grid=(rows // step,),
        in_specs=[grad_spec(slabs, 0, step), pl.BlockSpec((step, cols, cols), lambda i: (i, 0, 0)), row_spec, row_spec],
        out_specs=[row_spec, row_spec],
        out_shape=[row_shape, row_shape],
        compiler_params=params(24),
        cost_estimate=cost(4 * rows * cols * cols * d, 2 * rows * cols * (cols + 5 * d)),
    )(slabs, first_blocks, tokens, gate_values)


def column_pair(g_ref, k):
    devices, _, _, both, d = g_ref.shape
    pair = g_ref[:, 0, k].astype(F32).reshape(devices, 2, both // 2, d)
    return [pair[:, c].reshape(devices * both // 2, d).astype(BF16) for c in range(2)]


def second_terms(place, whose, slabs, cotangent):
    cols, rows, d = cotangent.shape
    devices, _, pairs, both, _ = slabs.shape
    step, part = pairs // 4, cols // 4

    def kernel(place_ref, g_ref, c_ref, out_ref):
        for k in range(step):
            for c, column in enumerate(column_pair(g_ref, k)):
                out_ref[0, 2 * k + c] = dot(c_ref[2 * k + c], column, NT).astype(BF16)

    def quarter(i, at):
        return jnp.where(i == 0, at[whose[0]], at[whose[1]])

    return pl.pallas_call(
        kernel,
        grid_spec=pltpu.PrefetchScalarGridSpec(
            num_scalar_prefetch=1,
            grid=(2,),
            in_specs=[
                pl.BlockSpec((devices, 1, step, both, d), lambda i, at: (0, GATED, quarter(i, at), 0, 0)),
                pl.BlockSpec((part, rows, d), lambda i, at: (quarter(i, at), 0, 0)),
            ],
            out_specs=pl.BlockSpec((1, part, rows, rows), lambda i, at: (i, 0, 0, 0)),
        ),
        out_shape=jax.ShapeDtypeStruct((2, part, rows, rows), BF16),
        compiler_params=params(24),
        cost_estimate=cost(cols * rows * rows * d, cols * rows * (rows + 2 * d)),
    )(place, slabs, cotangent)


def mixed_columns(slabs, second_blocks):
    cols, rows, _ = second_blocks.shape
    devices, _, pairs, both, d = slabs.shape
    step = 4

    def kernel(g_ref, s_ref, out_ref):
        for k in range(step):
            for c, column in enumerate(column_pair(g_ref, k)):
                out_ref[2 * k + c] = dot(s_ref[2 * k + c], column, NN).astype(BF16)

    return pl.pallas_call(
        kernel,
        grid=(pairs // step,),
        in_specs=[
            pl.BlockSpec((devices, 1, step, both, d), lambda i: (0, GATED, i, 0, 0)),
            pl.BlockSpec((2 * step, rows, rows), lambda i: (i, 0, 0)),
        ],
        out_specs=pl.BlockSpec((2 * step, rows, d), lambda i: (i, 0, 0)),
        out_shape=jax.ShapeDtypeStruct((cols, rows, d), BF16),
        compiler_params=params(24),
        cost_estimate=cost(2 * cols * rows * rows * d, 2 * cols * rows * (rows + 2 * d)),
    )(slabs, second_blocks)


def swap(x, bit):
    return lax.ppermute(x, "ch", [(i, i ^ bit) for i in range(4)])


def add(a, b):
    return a.astype(F32) + b.astype(F32)


def after(first, *later):
    return lax.optimization_barrier((first, *later))


def local(tokens, gate_values, first_blocks, second_blocks, cotangent):
    rows = tokens.shape[0]
    ch = lax.axis_index("ch")
    place = jnp.stack([ch, ch ^ 2, ch ^ 1, ch ^ 3]).astype(jnp.int32)

    slabs = send_slabs(second_blocks, cotangent, first_blocks, tokens, gate_values, lax.axis_size("seq"))
    slabs, place = after(slabs, place)
    slabs = lax.all_to_all(slabs, "seq", split_axis=0, concat_axis=0, tiled=True)

    def over_cores(near, far):
        return add(near[1], far[1]).astype(BF16)

    def over_chips(near, far, across):
        return (add(near[0], far[0]) + across.astype(F32)).astype(BF16)

    near_b, far_b = first_terms(place, slabs, tokens, gate_values, 0, rows)
    far_b = swap(far_b, 1)
    far_c = swap(second_terms(place, (BESIDE, OPPOSITE), slabs, cotangent), 1)
    near_c = second_terms(place, (HERE, ACROSS), slabs, cotangent)
    sum_b, sum_c = over_cores(near_b, far_b), over_cores(near_c, far_c)
    sum_b, sum_c, gate_values, second_blocks = after(sum_b, sum_c, gate_values, second_blocks)
    across_b, across_c = swap(sum_b, 2), swap(sum_c, 2)
    mixed_output = mixed_columns(slabs, second_blocks)
    token_grad, gate_grad = row_grads(slabs, first_blocks, tokens, gate_values)
    first_grad, second_grad = over_chips(near_b, far_b, across_b), over_chips(near_c, far_c, across_c)
    return (mixed_output, token_grad, gate_grad, first_grad, second_grad)


def solution(mesh):
    return jax.shard_map(
        local,
        mesh=mesh,
        in_specs=(
            P("seq", None, "ch"),
            P("seq", None, "ch"),
            P("seq", None, None),
            P("seq", None, None),
            P("seq", None, "ch"),
        ),
        out_specs=(
            P("seq", None, "ch"),
            P("seq", None, "ch"),
            P("seq", None, "ch"),
            P("seq", "ch", None),
            P(("seq", "ch"), None, None),
        ),
        check_vma=False,
    )
```

```python
import jax
import jax.numpy as jnp
from jax import lax
from jax.experimental import pallas as pl
from jax.experimental.pallas import tpu as pltpu
from jax.sharding import PartitionSpec as P

F32 = jnp.float32
BF16 = jnp.bfloat16
MIB = 1024 * 1024
LANES = 128
PAD = 1
SCALE = 100000

NN = (((1,), (0,)), ((), ()))
NT = (((1,), (1,)), ((), ()))
TN = (((0,), (0,)), ((), ()))

HERE, ACROSS, BESIDE, OPPOSITE = range(4)

GRAD, GATED = range(2)


def dot(a, b, dims):
    return lax.dot_general(a, b, dims, preferred_element_type=F32)


def params(mib=60):
    return pltpu.CompilerParams(vmem_limit_bytes=mib * MIB)


def cost(flops, nbytes):
    return pl.CostEstimate(flops=flops // SCALE, bytes_accessed=nbytes // SCALE, transcendentals=0)


def lanes(t):
    return slice(t * LANES, (t + 1) * LANES)


def send_slabs(second_blocks, cotangent, first_blocks, tokens, gate_values, devices):
    cols, all_rows, d = cotangent.shape
    rows, all_cols, _ = tokens.shape
    tiles, pairs = d // LANES, cols // 2
    chunk, span = 4, 128
    chunks, spans = cols // chunk, all_cols // span
    back_pitch, gated_pitch = all_rows + PAD, span + PAD

    def kernel(s_hbm, c_hbm, f_hbm, t_hbm, g_hbm, out_ref, s_ref, c_ref, f_ref, t_ref, g_ref, back, gated, sems):
        fetches = []

        def fetch(at, *sources_and_targets):
            for source, target in sources_and_targets:
                copy = pltpu.make_async_copy(source.at[at], target.at[at], sems.at[len(fetches)])
                copy.start()
                fetches.append(copy)

        def arrive(first, count):
            for copy in fetches[first:first + count]:
                copy.wait()

        for i in range(chunks):
            fetch(pl.ds(i * chunk, chunk), (s_hbm, s_ref), (c_hbm, c_ref))
        fetch(pl.ds(0, rows), (t_hbm, t_ref))
        for i in range(spans):
            fetch((pl.ds(0, rows), pl.ds(i * span, span)), (f_hbm, f_ref), (g_hbm, g_ref))

        for i in range(chunks):
            arrive(2 * i, 2)
            for c in range(i * chunk, (i + 1) * chunk):
                product = dot(s_ref[c], c_ref[c], TN)
                for t in range(tiles):
                    back[t, c * back_pitch:c * back_pitch + all_rows, :] = product[:, lanes(t)]

        def rows_of(k, carry):
            for r in range(rows):
                for t in range(tiles):
                    strip = back[t, pl.ds(k * rows + r, cols, stride=back_pitch), :]
                    out_ref[k, GRAD, r, :, lanes(t)] = strip.astype(BF16)
            return carry

        lax.fori_loop(0, devices, rows_of, 0, unroll=2)

        arrive(2 * chunks, 1)
        for i in range(spans):
            arrive(2 * chunks + 1 + 2 * i, 2)
            part = pl.ds(i * span, span)
            for r in range(rows):
                product = dot(f_ref[r, part, :], t_ref[r], NN) * g_ref[r, part, :].astype(F32)
                for t in range(tiles):
                    gated[t, r * gated_pitch:r * gated_pitch + span, :] = product[:, lanes(t)]

            def columns_of(k, carry):
                for j in range(pairs):
                    at = k * cols + 2 * j
                    for t in range(tiles):
                        even = gated[t, pl.ds(at, rows, stride=gated_pitch), :]
                        odd = gated[t, pl.ds(at + 1, rows, stride=gated_pitch), :]
                        pair = jnp.concatenate([even, odd], axis=0)
                        out_ref[i * (span // cols) + k, GATED, j, :, lanes(t)] = pair.astype(BF16)
                return carry

            lax.fori_loop(0, span // cols, columns_of, 0, unroll=2)

    hbm = pl.BlockSpec(memory_space=pltpu.HBM)
    return pl.pallas_call(
        kernel,
        in_specs=[hbm] * 5,
        out_specs=pl.BlockSpec(memory_space=pltpu.VMEM),
        out_shape=pltpu.VMEM((devices, 2, rows, cols, d), BF16),
        scratch_shapes=[
            pltpu.VMEM(second_blocks.shape, BF16),
            pltpu.VMEM(cotangent.shape, BF16),
            pltpu.VMEM(first_blocks.shape, BF16),
            pltpu.VMEM(tokens.shape, BF16),
            pltpu.VMEM(gate_values.shape, BF16),
            pltpu.VMEM((tiles, (cols + 1) * back_pitch + 7, LANES), F32),
            pltpu.VMEM((tiles, (rows + 1) * gated_pitch + 7, LANES), F32),
            pltpu.SemaphoreType.DMA((2 * chunks + 1 + 2 * spans,)),
        ],
        compiler_params=params(48),
        cost_estimate=cost(
            2 * cols * all_rows * all_rows * d + 2 * rows * all_cols * all_cols * d,
            2 * cols * all_rows * (all_rows + 2 * d) + 2 * rows * all_cols * (all_cols + 3 * d),
        ),
    )(second_blocks, cotangent, first_blocks, tokens, gate_values)


def grad_spec(slabs, step):
    devices, _, _, both, d = slabs.shape
    return pl.BlockSpec((devices, 1, step, both, d), lambda i: (0, GRAD, i, 0, 0))


def first_terms(place, whose, slabs, tokens, gate_values):
    rows, cols, d = tokens.shape
    part, step = cols // 4, 4

    def kernel(place_ref, b_ref, t_ref, g_ref, out_ref):
        for r in range(step):
            back = b_ref[:, 0, r].reshape(part, d).astype(F32)
            hidden_grad = (back * g_ref[r].astype(F32)).astype(BF16)
            out_ref[r] = dot(hidden_grad, t_ref[r], NT).astype(BF16)

    devices, _, _, both, _ = slabs.shape
    return pl.pallas_call(
        kernel,
        grid_spec=pltpu.PrefetchScalarGridSpec(
            num_scalar_prefetch=1,
            grid=(rows // step,),
            in_specs=[
                pl.BlockSpec((devices // 4, 1, step, both, d), lambda i, at: (at[whose], GRAD, i, 0, 0)),
                pl.BlockSpec((step, cols, d), lambda i, at: (i, 0, 0)),
                pl.BlockSpec((step, part, d), lambda i, at: (i, at[whose], 0)),
            ],
            out_specs=pl.BlockSpec((step, part, cols), lambda i, at: (i, 0, 0)),
        ),
        out_shape=jax.ShapeDtypeStruct((rows, part, cols), BF16),
        compiler_params=params(24),
        cost_estimate=cost(rows * cols * part * d * 2, 2 * rows * (cols * part + 2 * part * d + cols * d)),
    )(place, slabs, tokens, gate_values)


def row_grads(slabs, first_blocks, tokens, gate_values):
    rows, cols, d = tokens.shape

    step = 2

    def kernel(b_ref, f_ref, t_ref, g_ref, tg_ref, gg_ref):
        for k in range(step):
            back = b_ref[:, 0, k].reshape(cols, d).astype(F32)
            hidden_grad = (back * g_ref[k].astype(F32)).astype(BF16)
            tg_ref[k] = dot(f_ref[k], hidden_grad, TN).astype(BF16)
            gg_ref[k] = (back * dot(f_ref[k], t_ref[k], NN)).astype(BF16)

    row_spec = pl.BlockSpec((step, cols, d), lambda i: (i, 0, 0))
    row_shape = jax.ShapeDtypeStruct((rows, cols, d), BF16)
    return pl.pallas_call(
        kernel,
        grid=(rows // step,),
        in_specs=[grad_spec(slabs, step), pl.BlockSpec((step, cols, cols), lambda i: (i, 0, 0)), row_spec, row_spec],
        out_specs=[row_spec, row_spec],
        out_shape=[row_shape, row_shape],
        compiler_params=params(24),
        cost_estimate=cost(4 * rows * cols * cols * d, 2 * rows * cols * (cols + 5 * d)),
    )(slabs, first_blocks, tokens, gate_values)


def column_pair(g_ref, k):
    devices, _, _, both, d = g_ref.shape
    pair = g_ref[:, 0, k].astype(F32).reshape(devices, 2, both // 2, d)
    return [pair[:, c].reshape(devices * both // 2, d).astype(BF16) for c in range(2)]


def second_terms(place, whose, slabs, cotangent):
    cols, rows, d = cotangent.shape
    devices, _, pairs, both, _ = slabs.shape
    step, part = pairs // 4, cols // 4

    def kernel(place_ref, g_ref, c_ref, out_ref):
        for k in range(step):
            for c, column in enumerate(column_pair(g_ref, k)):
                out_ref[2 * k + c] = dot(c_ref[2 * k + c], column, NT).astype(BF16)

    return pl.pallas_call(
        kernel,
        grid_spec=pltpu.PrefetchScalarGridSpec(
            num_scalar_prefetch=1,
            grid=(1,),
            in_specs=[
                pl.BlockSpec((devices, 1, step, both, d), lambda i, at: (0, GATED, at[whose], 0, 0)),
                pl.BlockSpec((part, rows, d), lambda i, at: (at[whose], 0, 0)),
            ],
            out_specs=pl.BlockSpec((part, rows, rows), lambda i, at: (0, 0, 0)),
        ),
        out_shape=jax.ShapeDtypeStruct((part, rows, rows), BF16),
        compiler_params=params(24),
        cost_estimate=cost(2 * part * rows * rows * d, 2 * part * rows * (rows + 2 * d)),
    )(place, slabs, cotangent)


def mixed_columns(slabs, second_blocks):
    cols, rows, _ = second_blocks.shape
    devices, _, pairs, both, d = slabs.shape
    step = 4

    def kernel(g_ref, s_ref, out_ref):
        for k in range(step):
            for c, column in enumerate(column_pair(g_ref, k)):
                out_ref[2 * k + c] = dot(s_ref[2 * k + c], column, NN).astype(BF16)

    return pl.pallas_call(
        kernel,
        grid=(pairs // step,),
        in_specs=[
            pl.BlockSpec((devices, 1, step, both, d), lambda i: (0, GATED, i, 0, 0)),
            pl.BlockSpec((2 * step, rows, rows), lambda i: (i, 0, 0)),
        ],
        out_specs=pl.BlockSpec((2 * step, rows, d), lambda i: (i, 0, 0)),
        out_shape=jax.ShapeDtypeStruct((cols, rows, d), BF16),
        compiler_params=params(24),
        cost_estimate=cost(2 * cols * rows * rows * d, 2 * cols * rows * (rows + 2 * d)),
    )(slabs, second_blocks)


def swap(x, bit):
    return lax.ppermute(x, "ch", [(i, i ^ bit) for i in range(4)])


def add(a, b):
    return a.astype(F32) + b.astype(F32)


def after(first, *later):
    return lax.optimization_barrier((first, *later))


def local(tokens, gate_values, first_blocks, second_blocks, cotangent):
    ch = lax.axis_index("ch")
    place = jnp.stack([ch, ch ^ 2, ch ^ 1, ch ^ 3]).astype(jnp.int32)

    slabs = send_slabs(second_blocks, cotangent, first_blocks, tokens, gate_values, lax.axis_size("seq"))
    slabs, place = after(slabs, place)
    slabs = lax.all_to_all(slabs, "seq", split_axis=0, concat_axis=0, tiled=True)

    def terms(whose):
        return first_terms(place, whose, slabs, tokens, gate_values), second_terms(place, whose, slabs, cotangent)

    def over_cores(whose, whose_beside):
        first, second = terms(whose_beside)
        first, second = swap(first, 1), swap(second, 1)
        near_first, near_second = terms(whose)
        return add(near_first, first), add(near_second, second)

    away = [x.astype(BF16) for x in over_cores(ACROSS, OPPOSITE)]
    *away, second_blocks = after(*away, second_blocks)
    across_c, across_b = swap(away[1], 2), swap(away[0], 2)
    mixed_output = mixed_columns(slabs, second_blocks)
    across_c, mixed_output, tokens, gate_values, cotangent = after(
        across_c, mixed_output, tokens, gate_values, cotangent
    )
    here_b, here_c = over_cores(HERE, BESIDE)
    second_grad, gate_values = after((here_c + across_c.astype(F32)).astype(BF16), gate_values)
    token_grad, gate_grad = row_grads(slabs, first_blocks, tokens, gate_values)
    first_grad = (here_b + across_b.astype(F32)).astype(BF16)
    return (mixed_output, token_grad, gate_grad, first_grad, second_grad)


def solution(mesh):
    return jax.shard_map(
        local,
        mesh=mesh,
        in_specs=(
            P("seq", None, "ch"),
            P("seq", None, "ch"),
            P("seq", None, None),
            P("seq", None, None),
            P("seq", None, "ch"),
        ),
        out_specs=(
            P("seq", None, "ch"),
            P("seq", None, "ch"),
            P("seq", None, "ch"),
            P("seq", "ch", None),
            P(("seq", "ch"), None, None),
        ),
        check_vma=False,
    )
```

```python
import jax
import jax.numpy as jnp
from jax import lax
from jax.experimental import pallas as pl
from jax.experimental.pallas import tpu as pltpu
from jax.sharding import PartitionSpec as P

F32 = jnp.float32
BF16 = jnp.bfloat16
MIB = 1024 * 1024
LANES = 128
PAD = 1
SCALE = 100000

NN = (((1,), (0,)), ((), ()))
NT = (((1,), (1,)), ((), ()))
TN = (((0,), (0,)), ((), ()))

HERE, ACROSS, BESIDE, OPPOSITE = range(4)

GRAD, GATED = range(2)


def dot(a, b, dims):
    return lax.dot_general(a, b, dims, preferred_element_type=F32)


def params(mib=60):
    return pltpu.CompilerParams(vmem_limit_bytes=mib * MIB)


def cost(flops, nbytes):
    return pl.CostEstimate(flops=flops // SCALE, bytes_accessed=nbytes // SCALE, transcendentals=0)


def lanes(t):
    return slice(t * LANES, (t + 1) * LANES)


def send_slabs(second_blocks, cotangent, first_blocks, tokens, gate_values, devices):
    cols, all_rows, d = cotangent.shape
    rows, all_cols, _ = tokens.shape
    tiles, pairs = d // LANES, cols // 2
    chunk, span = 4, 128
    chunks, spans = cols // chunk, all_cols // span
    back_pitch, gated_pitch = all_rows + PAD, span + PAD

    def kernel(s_hbm, c_hbm, f_hbm, t_hbm, g_hbm, out_ref, s_ref, c_ref, f_ref, t_ref, g_ref, back, gated, sems):
        fetches = []

        def fetch(at, *sources_and_targets):
            for source, target in sources_and_targets:
                copy = pltpu.make_async_copy(source.at[at], target.at[at], sems.at[len(fetches)])
                copy.start()
                fetches.append(copy)

        def arrive(first, count):
            for copy in fetches[first:first + count]:
                copy.wait()

        for i in range(chunks):
            fetch(pl.ds(i * chunk, chunk), (s_hbm, s_ref), (c_hbm, c_ref))
        fetch(pl.ds(0, rows), (t_hbm, t_ref))
        for i in range(spans):
            fetch((pl.ds(0, rows), pl.ds(i * span, span)), (f_hbm, f_ref), (g_hbm, g_ref))

        for i in range(chunks):
            arrive(2 * i, 2)
            for c in range(i * chunk, (i + 1) * chunk):
                product = dot(s_ref[c], c_ref[c], TN)
                for t in range(tiles):
                    back[t, c * back_pitch:c * back_pitch + all_rows, :] = product[:, lanes(t)]

        def rows_of(k, carry):
            for r in range(rows):
                for t in range(tiles):
                    strip = back[t, pl.ds(k * rows + r, cols, stride=back_pitch), :]
                    out_ref[k, GRAD, r, :, lanes(t)] = strip.astype(BF16)
            return carry

        lax.fori_loop(0, devices, rows_of, 0, unroll=2)

        arrive(2 * chunks, 1)
        for i in range(spans):
            arrive(2 * chunks + 1 + 2 * i, 2)
            part = pl.ds(i * span, span)
            for r in range(rows):
                product = dot(f_ref[r, part, :], t_ref[r], NN) * g_ref[r, part, :].astype(F32)
                for t in range(tiles):
                    gated[t, r * gated_pitch:r * gated_pitch + span, :] = product[:, lanes(t)]

            def columns_of(k, carry):
                for j in range(pairs):
                    at = k * cols + 2 * j
                    for t in range(tiles):
                        even = gated[t, pl.ds(at, rows, stride=gated_pitch), :]
                        odd = gated[t, pl.ds(at + 1, rows, stride=gated_pitch), :]
                        pair = jnp.concatenate([even, odd], axis=0)
                        out_ref[i * (span // cols) + k, GATED, j, :, lanes(t)] = pair.astype(BF16)
                return carry

            lax.fori_loop(0, span // cols, columns_of, 0, unroll=2)

    hbm = pl.BlockSpec(memory_space=pltpu.HBM)
    return pl.pallas_call(
        kernel,
        in_specs=[hbm] * 5,
        out_specs=pl.BlockSpec(memory_space=pltpu.VMEM),
        out_shape=pltpu.VMEM((devices, 2, rows, cols, d), BF16),
        scratch_shapes=[
            pltpu.VMEM(second_blocks.shape, BF16),
            pltpu.VMEM(cotangent.shape, BF16),
            pltpu.VMEM(first_blocks.shape, BF16),
            pltpu.VMEM(tokens.shape, BF16),
            pltpu.VMEM(gate_values.shape, BF16),
            pltpu.VMEM((tiles, (cols + 1) * back_pitch + 7, LANES), F32),
            pltpu.VMEM((tiles, (rows + 1) * gated_pitch + 7, LANES), F32),
            pltpu.SemaphoreType.DMA((2 * chunks + 1 + 2 * spans,)),
        ],
        compiler_params=params(48),
        cost_estimate=cost(
            2 * cols * all_rows * all_rows * d + 2 * rows * all_cols * all_cols * d,
            2 * cols * all_rows * (all_rows + 2 * d) + 2 * rows * all_cols * (all_cols + 3 * d),
        ),
    )(second_blocks, cotangent, first_blocks, tokens, gate_values)


def grad_spec(slabs, step):
    devices, _, _, both, d = slabs.shape
    return pl.BlockSpec((devices, 1, step, both, d), lambda i: (0, GRAD, i, 0, 0))


def first_terms(place, whose, slabs, tokens, gate_values):
    rows, cols, d = tokens.shape
    devices, part = slabs.shape[0], cols // 4
    group, count = devices // 4, len(whose)

    def kernel(place_ref, b_ref, t_ref, g_ref, *rest):
        outs, held = rest[:count], rest[count]
        for r in range(rows):
            for k, name in enumerate(whose):
                at = place_ref[name]
                columns = pl.ds(pl.multiple_of(at * part, part), part)
                back = b_ref[pl.ds(at * group, group), GRAD, r].reshape(part, d).astype(F32)
                held[k * part:(k + 1) * part, :] = (back * g_ref[r, columns, :].astype(F32)).astype(BF16)
            terms = dot(held[...], t_ref[r], NT).astype(BF16)
            for k, out in enumerate(outs):
                out[r] = terms[k * part:(k + 1) * part]

    vmem = pl.BlockSpec(memory_space=pltpu.VMEM)
    return pl.pallas_call(
        kernel,
        in_specs=[pl.BlockSpec(memory_space=pltpu.SMEM), vmem, vmem, vmem],
        out_specs=[vmem] * count,
        out_shape=[pltpu.VMEM((rows, part, cols), BF16)] * count,
        scratch_shapes=[pltpu.VMEM((count * part, d), BF16)],
        compiler_params=params(8),
        cost_estimate=cost(count * rows * cols * part * d * 2, 2 * count * rows * (cols * part + 2 * part * d)),
    )(place, slabs, tokens, gate_values)


def row_grads(slabs, first_blocks, tokens, gate_values):
    rows, cols, d = tokens.shape

    step = 2

    def kernel(b_ref, f_ref, t_ref, g_ref, tg_ref, gg_ref):
        for k in range(step):
            back = b_ref[:, 0, k].reshape(cols, d).astype(F32)
            hidden_grad = (back * g_ref[k].astype(F32)).astype(BF16)
            tg_ref[k] = dot(f_ref[k], hidden_grad, TN).astype(BF16)
            gg_ref[k] = (back * dot(f_ref[k], t_ref[k], NN)).astype(BF16)

    row_spec = pl.BlockSpec((step, cols, d), lambda i: (i, 0, 0))
    row_shape = jax.ShapeDtypeStruct((rows, cols, d), BF16)
    return pl.pallas_call(
        kernel,
        grid=(rows // step,),
        in_specs=[grad_spec(slabs, step), pl.BlockSpec((step, cols, cols), lambda i: (i, 0, 0)), row_spec, row_spec],
        out_specs=[row_spec, row_spec],
        out_shape=[row_shape, row_shape],
        compiler_params=params(24),
        cost_estimate=cost(4 * rows * cols * cols * d, 2 * rows * cols * (cols + 5 * d)),
    )(slabs, first_blocks, tokens, gate_values)


def split_pair(pair):
    devices, both, d = pair.shape
    pair = pair.astype(F32).reshape(devices, 2, both // 2, d)
    return [pair[:, c].reshape(devices * both // 2, d).astype(BF16) for c in range(2)]


def second_terms(place, whose, slabs, cotangent):
    cols, rows, d = cotangent.shape
    _, _, pairs, _, _ = slabs.shape
    step, part = pairs // 4, cols // 4

    def kernel(place_ref, g_ref, c_ref, out_ref):
        at = place_ref[whose]
        for k in range(step):
            for c, column in enumerate(split_pair(g_ref[:, GATED, at * step + k])):
                out_ref[2 * k + c] = dot(c_ref[at * part + 2 * k + c], column, NT).astype(BF16)

    vmem = pl.BlockSpec(memory_space=pltpu.VMEM)
    return pl.pallas_call(
        kernel,
        in_specs=[pl.BlockSpec(memory_space=pltpu.SMEM), vmem, vmem],
        out_specs=vmem,
        out_shape=pltpu.VMEM((part, rows, rows), BF16),
        compiler_params=params(8),
        cost_estimate=cost(2 * part * rows * rows * d, 2 * part * rows * (rows + 2 * d)),
    )(place, slabs, cotangent)


def mixed_columns(slabs, second_blocks):
    cols, rows, _ = second_blocks.shape
    devices, _, pairs, both, d = slabs.shape
    step = 4

    def kernel(g_ref, s_ref, out_ref):
        for k in range(step):
            for c, column in enumerate(split_pair(g_ref[:, 0, k])):
                out_ref[2 * k + c] = dot(s_ref[2 * k + c], column, NN).astype(BF16)

    return pl.pallas_call(
        kernel,
        grid=(pairs // step,),
        in_specs=[
            pl.BlockSpec((devices, 1, step, both, d), lambda i: (0, GATED, i, 0, 0)),
            pl.BlockSpec((2 * step, rows, rows), lambda i: (i, 0, 0)),
        ],
        out_specs=pl.BlockSpec((2 * step, rows, d), lambda i: (i, 0, 0)),
        out_shape=jax.ShapeDtypeStruct((cols, rows, d), BF16),
        compiler_params=params(24),
        cost_estimate=cost(2 * cols * rows * rows * d, 2 * cols * rows * (rows + 2 * d)),
    )(slabs, second_blocks)


def swap(x, bit):
    return lax.ppermute(x, "ch", [(i, i ^ bit) for i in range(4)])


def add(a, b):
    return a.astype(F32) + b.astype(F32)


def after(first, *later):
    return lax.optimization_barrier((first, *later))


def local(tokens, gate_values, first_blocks, second_blocks, cotangent):
    ch = lax.axis_index("ch")
    place = jnp.stack([ch, ch ^ 2, ch ^ 1, ch ^ 3]).astype(jnp.int32)

    slabs = send_slabs(second_blocks, cotangent, first_blocks, tokens, gate_values, lax.axis_size("seq"))
    slabs, place = after(slabs, place)
    slabs = lax.all_to_all(slabs, "seq", split_axis=0, concat_axis=0, tiled=True)

    def over_cores(whose, whose_beside):
        first, near_first = first_terms(place, (whose_beside, whose), slabs, tokens, gate_values)
        first, late = after(first, cotangent)
        first = swap(first, 1)
        second = swap(second_terms(place, whose_beside, slabs, late), 1)
        near_second = second_terms(place, whose, slabs, late)
        return add(near_first, first), add(near_second, second)

    away = [x.astype(BF16) for x in over_cores(ACROSS, OPPOSITE)]
    *away, second_blocks = after(*away, second_blocks)
    across_c, across_b = swap(away[1], 2), swap(away[0], 2)
    mixed_output = mixed_columns(slabs, second_blocks)
    across_c, mixed_output, tokens, gate_values, cotangent = after(
        across_c, mixed_output, tokens, gate_values, cotangent
    )
    here_b, here_c = over_cores(HERE, BESIDE)
    second_grad, gate_values = after((here_c + across_c.astype(F32)).astype(BF16), gate_values)
    token_grad, gate_grad = row_grads(slabs, first_blocks, tokens, gate_values)
    first_grad = (here_b + across_b.astype(F32)).astype(BF16)
    return (mixed_output, token_grad, gate_grad, first_grad, second_grad)


def solution(mesh):
    return jax.shard_map(
        local,
        mesh=mesh,
        in_specs=(
            P("seq", None, "ch"),
            P("seq", None, "ch"),
            P("seq", None, None),
            P("seq", None, None),
            P("seq", None, "ch"),
        ),
        out_specs=(
            P("seq", None, "ch"),
            P("seq", None, "ch"),
            P("seq", None, "ch"),
            P("seq", "ch", None),
            P(("seq", "ch"), None, None),
        ),
        check_vma=False,
    )
```

```python
import jax
import jax.numpy as jnp
from jax import lax
from jax.experimental import pallas as pl
from jax.experimental.pallas import tpu as pltpu
from jax.sharding import PartitionSpec as P

F32 = jnp.float32
BF16 = jnp.bfloat16
MIB = 1024 * 1024
LANES = 128
PAD = 1
SCALE = 100000

NN = (((1,), (0,)), ((), ()))
NT = (((1,), (1,)), ((), ()))
TN = (((0,), (0,)), ((), ()))

HERE, ACROSS, BESIDE, OPPOSITE = range(4)

GRAD, GATED = range(2)


def dot(a, b, dims):
    return lax.dot_general(a, b, dims, preferred_element_type=F32)


def params(mib=60):
    return pltpu.CompilerParams(vmem_limit_bytes=mib * MIB)


def cost(flops, nbytes):
    return pl.CostEstimate(flops=flops // SCALE, bytes_accessed=nbytes // SCALE, transcendentals=0)


def lanes(t):
    return slice(t * LANES, (t + 1) * LANES)


def send_slabs(second_blocks, cotangent, first_blocks, tokens, gate_values, devices):
    cols, all_rows, d = cotangent.shape
    rows, all_cols, _ = tokens.shape
    tiles, pairs = d // LANES, cols // 2
    chunk, span = 4, 128
    chunks, spans = cols // chunk, all_cols // span
    back_pitch, gated_pitch = all_rows + PAD, span + PAD

    def kernel(s_hbm, c_hbm, f_hbm, t_hbm, g_hbm, out_ref, s_ref, c_ref, f_ref, t_ref, g_ref, back, gated, sems):
        fetches = []

        def fetch(at, *sources_and_targets):
            for source, target in sources_and_targets:
                copy = pltpu.make_async_copy(source.at[at], target.at[at], sems.at[len(fetches)])
                copy.start()
                fetches.append(copy)

        def arrive(first, count):
            for copy in fetches[first:first + count]:
                copy.wait()

        for i in range(chunks):
            fetch(pl.ds(i * chunk, chunk), (s_hbm, s_ref), (c_hbm, c_ref))
        fetch(pl.ds(0, rows), (t_hbm, t_ref))
        for i in range(spans):
            fetch((pl.ds(0, rows), pl.ds(i * span, span)), (f_hbm, f_ref), (g_hbm, g_ref))

        for i in range(chunks):
            arrive(2 * i, 2)
            for c in range(i * chunk, (i + 1) * chunk):
                product = dot(s_ref[c], c_ref[c], TN)
                for t in range(tiles):
                    back[t, c * back_pitch:c * back_pitch + all_rows, :] = product[:, lanes(t)]

        def rows_of(k, carry):
            for r in range(rows):
                for t in range(tiles):
                    strip = back[t, pl.ds(k * rows + r, cols, stride=back_pitch), :]
                    out_ref[k, GRAD, r, :, lanes(t)] = strip.astype(BF16)
            return carry

        lax.fori_loop(0, devices, rows_of, 0, unroll=2)

        arrive(2 * chunks, 1)
        for i in range(spans):
            arrive(2 * chunks + 1 + 2 * i, 2)
            part = pl.ds(i * span, span)
            for r in range(rows):
                product = dot(f_ref[r, part, :], t_ref[r], NN) * g_ref[r, part, :].astype(F32)
                for t in range(tiles):
                    gated[t, r * gated_pitch:r * gated_pitch + span, :] = product[:, lanes(t)]

            def columns_of(k, carry):
                for j in range(pairs):
                    at = k * cols + 2 * j
                    for t in range(tiles):
                        even = gated[t, pl.ds(at, rows, stride=gated_pitch), :]
                        odd = gated[t, pl.ds(at + 1, rows, stride=gated_pitch), :]
                        pair = jnp.concatenate([even, odd], axis=0)
                        out_ref[i * (span // cols) + k, GATED, j, :, lanes(t)] = pair.astype(BF16)
                return carry

            lax.fori_loop(0, span // cols, columns_of, 0, unroll=2)

    hbm = pl.BlockSpec(memory_space=pltpu.HBM)
    return pl.pallas_call(
        kernel,
        in_specs=[hbm] * 5,
        out_specs=pl.BlockSpec(memory_space=pltpu.VMEM),
        out_shape=pltpu.VMEM((devices, 2, rows, cols, d), BF16),
        scratch_shapes=[
            pltpu.VMEM(second_blocks.shape, BF16),
            pltpu.VMEM(cotangent.shape, BF16),
            pltpu.VMEM(first_blocks.shape, BF16),
            pltpu.VMEM(tokens.shape, BF16),
            pltpu.VMEM(gate_values.shape, BF16),
            pltpu.VMEM((tiles, (cols + 1) * back_pitch + 7, LANES), F32),
            pltpu.VMEM((tiles, (rows + 1) * gated_pitch + 7, LANES), F32),
            pltpu.SemaphoreType.DMA((2 * chunks + 1 + 2 * spans,)),
        ],
        compiler_params=params(48),
        cost_estimate=cost(
            2 * cols * all_rows * all_rows * d + 2 * rows * all_cols * all_cols * d,
            2 * cols * all_rows * (all_rows + 2 * d) + 2 * rows * all_cols * (all_cols + 3 * d),
        ),
    )(second_blocks, cotangent, first_blocks, tokens, gate_values)


def grad_spec(slabs, step):
    devices, _, _, both, d = slabs.shape
    return pl.BlockSpec((devices, 1, step, both, d), lambda i: (0, GRAD, i, 0, 0))


def first_terms(place, whose, slabs, tokens, gate_values):
    rows, cols, d = tokens.shape
    devices, part = slabs.shape[0], cols // 4
    group, count = devices // 4, len(whose)

    def kernel(place_ref, b_ref, t_ref, g_ref, *rest):
        outs, held = rest[:count], rest[count]
        for r in range(rows):
            for k, name in enumerate(whose):
                at = place_ref[name]
                columns = pl.ds(pl.multiple_of(at * part, part), part)
                back = b_ref[pl.ds(at * group, group), GRAD, r].reshape(part, d).astype(F32)
                held[k * part:(k + 1) * part, :] = (back * g_ref[r, columns, :].astype(F32)).astype(BF16)
            terms = dot(held[...], t_ref[r], NT).astype(BF16)
            for k, out in enumerate(outs):
                out[r] = terms[k * part:(k + 1) * part]

    vmem = pl.BlockSpec(memory_space=pltpu.VMEM)
    return pl.pallas_call(
        kernel,
        in_specs=[pl.BlockSpec(memory_space=pltpu.SMEM), vmem, vmem, vmem],
        out_specs=[vmem] * count,
        out_shape=[pltpu.VMEM((rows, part, cols), BF16)] * count,
        scratch_shapes=[pltpu.VMEM((count * part, d), BF16)],
        compiler_params=params(8),
        cost_estimate=cost(count * rows * cols * part * d * 2, 2 * count * rows * (cols * part + 2 * part * d)),
    )(place, slabs, tokens, gate_values)


def row_grads(slabs, first_blocks, tokens, gate_values):
    rows, cols, d = tokens.shape

    step = 2

    def kernel(b_ref, f_ref, t_ref, g_ref, tg_ref, gg_ref):
        for k in range(step):
            back = b_ref[:, 0, k].reshape(cols, d).astype(F32)
            hidden_grad = (back * g_ref[k].astype(F32)).astype(BF16)
            tg_ref[k] = dot(f_ref[k], hidden_grad, TN).astype(BF16)
            gg_ref[k] = (back * dot(f_ref[k], t_ref[k], NN)).astype(BF16)

    row_spec = pl.BlockSpec((step, cols, d), lambda i: (i, 0, 0))
    row_shape = jax.ShapeDtypeStruct((rows, cols, d), BF16)
    return pl.pallas_call(
        kernel,
        grid=(rows // step,),
        in_specs=[grad_spec(slabs, step), pl.BlockSpec((step, cols, cols), lambda i: (i, 0, 0)), row_spec, row_spec],
        out_specs=[row_spec, row_spec],
        out_shape=[row_shape, row_shape],
        compiler_params=params(24),
        cost_estimate=cost(4 * rows * cols * cols * d, 2 * rows * cols * (cols + 5 * d)),
    )(slabs, first_blocks, tokens, gate_values)


def split_pair(pair):
    devices, both, d = pair.shape
    pair = pair.astype(F32).reshape(devices, 2, both // 2, d)
    return [pair[:, c].reshape(devices * both // 2, d).astype(BF16) for c in range(2)]


def second_terms(place, whose, slabs, cotangent):
    cols, rows, d = cotangent.shape
    _, _, pairs, _, _ = slabs.shape
    step, part = pairs // 4, cols // 4

    def kernel(place_ref, g_ref, c_ref, out_ref):
        at = place_ref[whose]
        for k in range(step):
            for c, column in enumerate(split_pair(g_ref[:, GATED, at * step + k])):
                out_ref[2 * k + c] = dot(c_ref[at * part + 2 * k + c], column, NT).astype(BF16)

    vmem = pl.BlockSpec(memory_space=pltpu.VMEM)
    return pl.pallas_call(
        kernel,
        in_specs=[pl.BlockSpec(memory_space=pltpu.SMEM), vmem, vmem],
        out_specs=vmem,
        out_shape=pltpu.VMEM((part, rows, rows), BF16),
        compiler_params=params(8),
        cost_estimate=cost(2 * part * rows * rows * d, 2 * part * rows * (rows + 2 * d)),
    )(place, slabs, cotangent)


def mixed_columns(slabs, second_blocks):
    cols, rows, _ = second_blocks.shape
    devices, _, pairs, both, d = slabs.shape
    step = 4

    def kernel(g_ref, s_ref, out_ref):
        for k in range(step):
            for c, column in enumerate(split_pair(g_ref[:, 0, k])):
                out_ref[2 * k + c] = dot(s_ref[2 * k + c], column, NN).astype(BF16)

    return pl.pallas_call(
        kernel,
        grid=(pairs // step,),
        in_specs=[
            pl.BlockSpec((devices, 1, step, both, d), lambda i: (0, GATED, i, 0, 0)),
            pl.BlockSpec((2 * step, rows, rows), lambda i: (i, 0, 0)),
        ],
        out_specs=pl.BlockSpec((2 * step, rows, d), lambda i: (i, 0, 0)),
        out_shape=jax.ShapeDtypeStruct((cols, rows, d), BF16),
        compiler_params=params(24),
        cost_estimate=cost(2 * cols * rows * rows * d, 2 * cols * rows * (rows + 2 * d)),
    )(slabs, second_blocks)


def swap(x, bit):
    return lax.ppermute(x, "ch", [(i, i ^ bit) for i in range(4)])


def near_sum(near, beside):
    vmem = pl.BlockSpec(memory_space=pltpu.VMEM)

    def kernel(a_ref, b_ref, out_ref):
        for r in range(near.shape[0]):
            out_ref[r] = add(a_ref[r], b_ref[r])

    return pl.pallas_call(
        kernel,
        in_specs=[vmem] * 2,
        out_specs=vmem,
        out_shape=pltpu.VMEM(near.shape, F32),
        compiler_params=params(8),
        cost_estimate=cost(near.size, 8 * near.size),
    )(near, beside)


def add(a, b):
    return a.astype(F32) + b.astype(F32)


def after(first, *later):
    return lax.optimization_barrier((first, *later))


def local(tokens, gate_values, first_blocks, second_blocks, cotangent):
    ch = lax.axis_index("ch")
    place = jnp.stack([ch, ch ^ 2, ch ^ 1, ch ^ 3]).astype(jnp.int32)

    slabs = send_slabs(second_blocks, cotangent, first_blocks, tokens, gate_values, lax.axis_size("seq"))
    slabs, place = after(slabs, place)
    slabs = lax.all_to_all(slabs, "seq", split_axis=0, concat_axis=0, tiled=True)

    def over_cores(whose, whose_beside):
        first, near_first = first_terms(place, (whose_beside, whose), slabs, tokens, gate_values)
        first, late = after(first, cotangent)
        first = swap(first, 1)
        second = swap(second_terms(place, whose_beside, slabs, late), 1)
        near_second = second_terms(place, whose, slabs, late)
        return (near_first, first), add(near_second, second)

    first, second = over_cores(ACROSS, OPPOSITE)
    away = [add(*first).astype(BF16), second.astype(BF16)]
    *away, second_blocks = after(*away, second_blocks)
    across_c, across_b = swap(away[1], 2), swap(away[0], 2)
    mixed_output = mixed_columns(slabs, second_blocks)
    across_c, mixed_output, tokens, gate_values, cotangent = after(
        across_c, mixed_output, tokens, gate_values, cotangent
    )
    here_b, here_c = over_cores(HERE, BESIDE)
    here_b = near_sum(*here_b)
    second_grad, here_b, gate_values = after((here_c + across_c.astype(F32)).astype(BF16), here_b, gate_values)
    token_grad, gate_grad = row_grads(slabs, first_blocks, tokens, gate_values)
    first_grad = (here_b + across_b.astype(F32)).astype(BF16)
    return (mixed_output, token_grad, gate_grad, first_grad, second_grad)


def solution(mesh):
    return jax.shard_map(
        local,
        mesh=mesh,
        in_specs=(
            P("seq", None, "ch"),
            P("seq", None, "ch"),
            P("seq", None, None),
            P("seq", None, None),
            P("seq", None, "ch"),
        ),
        out_specs=(
            P("seq", None, "ch"),
            P("seq", None, "ch"),
            P("seq", None, "ch"),
            P("seq", "ch", None),
            P(("seq", "ch"), None, None),
        ),
        check_vma=False,
    )
```
